256 devices in a mesh: row: 16 (over z, x_hi), col: 16 (over x_lo, y, core).
Axes of the slice: x: 4 (x_hi: 2, x_lo: 2; x = x_hi * 2 + x_lo), y: 4, z: 8, core: 2. Of those that a mesh axis runs over, the one named last changes fastest.
Arguments:
- activations: bfloat16 [2048, 12288], P('row', 'col'), may hold values from -6 to 6
- out_grad: bfloat16 [2048, 12288], P('row', 'col'), may hold values from -6 to 6
- pre_act: bfloat16 [2048, 24576], P('col', 'row'), may hold values from -8 to 8
- w_in: bfloat16 [12288, 24576], P('col', 'row'), may hold values from -0.0546875 to 0.0546875
- w_out: bfloat16 [24576, 12288], P('row', 'col'), may hold values from -0.0390625 to 0.0390625
Outputs:
- grad_input: bfloat16 [2048, 12288], P('row', 'col')
- grad_w_in: bfloat16 [12288, 24576], P('col', 'row')
The draws below stay inside these ranges and needn't reach their ends.
All inputs are finite; a program needn't handle non-finite values.
Results may differ from the reference program's by a relative error of at most 0.04.
Values may be sent and summed in bfloat16 or wider, within the bound.
No kernel may reach another device: no remote copies, remote signals or barrier semaphores. Data moves between devices by JAX's collectives and lax.ppermute only.
A program may use at most 64 MiB of HBM per device.

```python
import math
import jax
import jax.numpy as jnp
from jax import lax

D = 12288
FF = 24576
TOKENS = 2048
N_ROW = 16
N_COL = 16


def block_levels(key, extent, split, smallest, largest):
    def one(axis_at, parts):
        heights = jax.random.uniform(jax.random.fold_in(jax.random.fold_in(key, 6), axis_at), (parts,), jnp.float32, smallest / len(split), largest / len(split))
        return jnp.repeat(jnp.exp(heights), extent[axis_at] // parts).reshape((-1,) + (1,) * (len(extent) - axis_at - 1))

    gain = one(*split[0])
    for cut in split[1:]:
        gain = gain * one(*cut)
    return gain


def gaussian(stream_key, shape, scale, most, shards=(), dtype=jnp.bfloat16):
    drawn = jax.random.normal(stream_key, shape, jnp.float32) * scale
    if len(shards) > 0:
        drawn = block_levels(stream_key, shape, shards, -0.22, 0.18) * drawn
    return jnp.clip(drawn, min=-most, max=most).astype(dtype)


def setup_inputs(seed: int = 0) -> dict:
    splits = jax.random.split(jax.random.key(seed), 6)
    activations = gaussian(splits[0], (TOKENS, D), 1.0, 6.0, ((0, 16), (1, 16)))
    out_grad = gaussian(splits[1], (TOKENS, D), 1.0, 6.0, ((0, 16), (1, 16)))
    pre_act = gaussian(splits[2], (TOKENS, FF), 1.5, 8.0, ((0, 16), (1, 16)))
    w_in = gaussian(splits[3], (D, FF), D ** -0.5, 0.0546875, ((0, 16), (1, 16)))
    w_out = gaussian(splits[4], (FF, D), FF ** -0.5, 0.0390625, ((0, 16), (1, 16)))
    return dict(activations=activations, out_grad=out_grad, pre_act=pre_act, w_in=w_in, w_out=w_out)


def gelu_slope(hidden):
    coeff = math.sqrt(2.0 / math.pi)
    inner = coeff * (hidden + 0.044715 * hidden * hidden * hidden)
    tanh_val = jnp.tanh(inner)
    return 0.5 * (1.0 + tanh_val) + 0.5 * hidden * (1.0 - tanh_val * tanh_val) * coeff * (1.0 + 3.0 * 0.044715 * hidden * hidden)

def blocked_sum(left, right, blocks):
    rows_left = left.shape[0]
    rows_right = right.shape[0]
    width = left.shape[1] // blocks
    left_blocks = jnp.transpose(left.reshape(rows_left, blocks, width), (1, 0, 2))
    right_blocks = jnp.transpose(right.reshape(rows_right, blocks, width), (1, 0, 2))

    def accumulate(total, pair):
        left_part, right_part = pair
        partial_val = jnp.dot(left_part, right_part.T, preferred_element_type=jnp.float32)
        rounded = lax.optimization_barrier(partial_val.astype(jnp.bfloat16))
        return (total + rounded.astype(jnp.float32), None)
    start = jnp.zeros((rows_left, rows_right), jnp.float32)
    total, unused = lax.scan(accumulate, start, (left_blocks, right_blocks))
    return total

def reference(activations, out_grad, pre_act, w_in, w_out):
    grad_act = blocked_sum(out_grad, w_out, N_COL)
    slope_val = gelu_slope(pre_act.astype(jnp.float32))
    hidden_grad = (grad_act * slope_val).astype(jnp.bfloat16)
    grad_input = blocked_sum(hidden_grad, w_in, N_ROW).astype(jnp.bfloat16)
    grad_w_in = jnp.dot(activations.T, hidden_grad, preferred_element_type=jnp.float32).astype(jnp.bfloat16)
    return (grad_input, grad_w_in)
```

```python
import math

import jax
import jax.numpy as jnp
from jax import lax
from jax.sharding import PartitionSpec as P

NZ, NH, NL, NY, NC = 8, 2, 2, 4, 2
TOK = 128
SUB = 8
CHUNKS = ((0, 1, -1), (2, -2, 3, -3, 4))


def gelu_slope(hidden):
    coeff = math.sqrt(2.0 / math.pi)
    inner = coeff * (hidden + 0.044715 * hidden * hidden * hidden)
    tanh_val = jnp.tanh(inner)
    return 0.5 * (1.0 + tanh_val) + 0.5 * hidden * (1.0 - tanh_val * tanh_val) * coeff * (
        1.0 + 3.0 * 0.044715 * hidden * hidden
    )


def times_trans(left, right):
    return lax.dot_general(
        left, right, (((left.ndim - 1,), (1,)), ((), ())), preferred_element_type=jnp.float32
    )


def trans_times(left, right):
    return lax.dot_general(
        left, right, (((0,), (0,)), ((), ())), preferred_element_type=jnp.float32
    )


def f32(x):
    return x.astype(jnp.float32)


def bf16(x):
    return x.astype(jnp.bfloat16)


def send_z(x, step):
    pairs = [
        (z * NH + h, (z + step) % NZ * NH + h) for z in range(NZ) for h in range(NH)
    ]
    return lax.ppermute(x, "row", pairs)


def swap_h(x):
    return lax.ppermute(x, "row", [(r, r ^ 1) for r in range(NZ * NH)])


def send_y(x, step):
    pairs = [
        ((l * NY + y) * NC + c, (l * NY + (y + step) % NY) * NC + c)
        for l in range(NL)
        for y in range(NY)
        for c in range(NC)
    ]
    return lax.ppermute(x, "col", pairs)


def swap_l(x):
    return lax.ppermute(x, "col", [(j, j ^ (NY * NC)) for j in range(NL * NY * NC)])


def swap_c(x):
    return lax.ppermute(x, "col", [(j, j ^ 1) for j in range(NL * NY * NC)])


def roll_to(x, start):
    twice = jnp.concatenate([x, x], axis=0)
    return lax.dynamic_slice_in_dim(twice, start, x.shape[0], axis=0)


def flip_if(x, flag, axis):
    return jnp.where(flag == 1, jnp.flip(x, axis), x)


def to_relative(x, l, y, c):
    x = x.reshape(NL, NY, NC, SUB, -1)
    x = flip_if(flip_if(x, l, 0), c, 2)
    x = roll_to(x.transpose(1, 2, 0, 3, 4), y)
    return x.transpose(1, 2, 0, 3, 4).reshape(TOK, -1)


def from_relative(x, l, y, c):
    x = x.reshape(NC, NL, NY, SUB, -1).transpose(2, 0, 1, 3, 4)
    x = roll_to(x, (NY - y) % NY).transpose(2, 0, 1, 3, 4)
    return flip_if(flip_if(x, l, 0), c, 2).reshape(TOK, -1)


def local(activations, out_grad, pre_act, w_in, w_out):
    row, col = lax.axis_index("row"), lax.axis_index("col")
    z, h = row // NH, row % NH
    l, y, c = col // (NY * NC), col // NC % NY, col % NC
    width, hid = activations.shape[1], w_in.shape[1]

    own = {0: to_relative(out_grad, l, y, c)}
    for step in (1, 2, 3):
        own[-step] = send_z(own[1 - step], 1)
        own[step] = send_z(own[step - 1], -1)
    half = TOK // 2
    own[4] = jnp.concatenate([send_z(own[-3][:half], 1), send_z(own[3][half:], -1)], axis=0)
    other = {}
    for group in ((0,), (1, -1), (2, -2), (3, -3), (4,)):
        got = swap_h(jnp.stack([own[d] for d in group]))
        for at, d in enumerate(group):
            other[d] = got[at]

    act = to_relative(activations, l, y, c)
    act = jnp.concatenate([act, swap_h(act)], axis=0)
    groups = [[zz * NH + hh for zz in range(NZ)] for hh in range(NH)]
    act_all = lax.all_gather(act, "row", axis_index_groups=groups, axis=0, tiled=True)
    act_all = act_all.reshape(NZ, NH * TOK, width)

    pre = lax.all_to_all(pre_act, "col", split_axis=0, concat_axis=0, tiled=True)
    pre = roll_to(pre.reshape(NZ, NH, SUB, hid), z)
    pre = flip_if(pre, h, 1)

    w_grad = None
    share = {}
    for chunk in CHUNKS:
        n = NH * len(chunk)
        x = jnp.stack([v[d] for d in chunk for v in (own, other)])
        x = x.reshape(n, NC, NL * NY * SUB, width)
        away = bf16(times_trans(x[:, 1], w_out))
        away = swap_c(away)
        part = bf16(times_trans(x[:, 0], w_out) + f32(away)).reshape(n, NL, NY, SUB, hid)
        total = f32(part[:, :, 0])
        for step in (2, 1, 3):
            total = total + f32(send_y(part[:, :, step], step))
        total = bf16(total)
        grad_act = f32(total[:, 0]) + f32(swap_l(total[:, 1]))
        slope = gelu_slope(f32(jnp.concatenate([pre[d % NZ] for d in chunk], axis=0)))
        hidden = bf16(grad_act * slope)

        pair = jnp.stack([hidden, swap_l(hidden)], axis=1)
        whole = [pair] + [send_y(pair, step) for step in (3, 2, 1)]
        whole = jnp.stack(whole, axis=2)
        whole = jnp.stack([whole, swap_c(whole)], axis=1).reshape(n * TOK, hid)

        x_grad = bf16(times_trans(whole, w_in)).reshape(len(chunk), NH, TOK, width)
        got = swap_h(x_grad[:, 1])
        for at, d in enumerate(chunk):
            share[d] = f32(x_grad[at, 0]) + f32(got[at])

        act_here = jnp.concatenate(
            [lax.dynamic_index_in_dim(act_all, (z + d) % NZ, 0, keepdims=False) for d in chunk], axis=0
        )
        term = trans_times(act_here, whole)
        w_grad = term if w_grad is None else w_grad + term

    up = send_z(bf16(share[4][:half]), 1)
    down = send_z(bf16(share[4][half:]), -1)
    rest = jnp.zeros((half, width), jnp.float32)
    up = f32(jnp.concatenate([up, bf16(rest)], axis=0))
    down = f32(jnp.concatenate([bf16(rest), down], axis=0))
    for d in (3, 2, 1):
        up = f32(send_z(bf16(share[d] + up), 1))
        down = f32(send_z(bf16(share[-d] + down), -1))
    grad_input = from_relative(bf16(share[0] + up + down), l, y, c)
    return (grad_input, bf16(w_grad))


def solution(mesh):
    in_specs = (P("row", "col"), P("row", "col"), P("col", "row"), P("col", "row"), P("row", "col"))
    out_specs = (P("row", "col"), P("col", "row"))
    return jax.shard_map(local, mesh=mesh, in_specs=in_specs, out_specs=out_specs, check_vma=False)
```

```python
import math

import jax
import jax.numpy as jnp
from jax import lax
from jax.sharding import PartitionSpec as P

NZ, NH, NL, NY, NC = 8, 2, 2, 4, 2
TOK = 128
SUB = 8
NEAR, FAR = (0, 1, -1, 2), (-2, 3, -3, 4)


def gelu_slope(hidden):
    coeff = math.sqrt(2.0 / math.pi)
    inner = coeff * (hidden + 0.044715 * hidden * hidden * hidden)
    tanh_val = jnp.tanh(inner)
    return 0.5 * (1.0 + tanh_val) + 0.5 * hidden * (1.0 - tanh_val * tanh_val) * coeff * (
        1.0 + 3.0 * 0.044715 * hidden * hidden
    )


def times_trans(left, right):
    return lax.dot_general(
        left, right, (((left.ndim - 1,), (1,)), ((), ())), preferred_element_type=jnp.float32
    )


def trans_times(left, right):
    return lax.dot_general(
        left, right, (((0,), (0,)), ((), ())), preferred_element_type=jnp.float32
    )


def f32(x):
    return x.astype(jnp.float32)


def bf16(x):
    return x.astype(jnp.bfloat16)


def send_z(x, step):
    pairs = [
        (z * NH + h, (z + step) % NZ * NH + h) for z in range(NZ) for h in range(NH)
    ]
    return lax.ppermute(x, "row", pairs)


def swap_h(x):
    return lax.ppermute(x, "row", [(r, r ^ 1) for r in range(NZ * NH)])


def send_y(x, step):
    pairs = [
        ((l * NY + y) * NC + c, (l * NY + (y + step) % NY) * NC + c)
        for l in range(NL)
        for y in range(NY)
        for c in range(NC)
    ]
    return lax.ppermute(x, "col", pairs)


def swap_l(x):
    return lax.ppermute(x, "col", [(j, j ^ (NY * NC)) for j in range(NL * NY * NC)])


def swap_c(x):
    return lax.ppermute(x, "col", [(j, j ^ 1) for j in range(NL * NY * NC)])


def after(x, *deps):
    return lax.optimization_barrier((x,) + deps)[0]


def roll_to(x, start):
    twice = jnp.concatenate([x, x], axis=0)
    return lax.dynamic_slice_in_dim(twice, start, x.shape[0], axis=0)


def flip_if(x, flag, axis):
    return jnp.where(flag == 1, jnp.flip(x, axis), x)


def to_relative(x, l, y, c):
    x = x.reshape(NL, NY, NC, SUB, -1)
    x = flip_if(flip_if(x, l, 0), c, 2)
    x = roll_to(x.transpose(1, 0, 2, 3, 4), y)
    return x.transpose(2, 0, 1, 3, 4).reshape(TOK, -1)


def from_relative(x, l, y, c):
    x = x.reshape(NC, NY, NL, SUB, -1).transpose(1, 2, 0, 3, 4)
    x = roll_to(x, (NY - y) % NY).transpose(1, 0, 2, 3, 4)
    return flip_if(flip_if(x, l, 0), c, 2).reshape(TOK, -1)


def sync(*xs):
    return lax.optimization_barrier(xs)


def local(activations, out_grad, pre_act, w_in, w_out):
    row, col = lax.axis_index("row"), lax.axis_index("col")
    z, h = row // NH, row % NH
    l, y, c = col // (NY * NC), col // NC % NY, col % NC
    width, hid = activations.shape[1], w_in.shape[1]
    mid = TOK // 2

    def ring_step(ring, step):
        if step < 4:
            return send_z(ring[1 - step], 1), send_z(ring[step - 1], -1)
        return send_z(ring[-3][:, :mid], 1), send_z(ring[3][:, mid:], -1)

    def keep(ring, step, got):
        if step < 4:
            ring[-step], ring[step] = got
        else:
            ring[4] = jnp.concatenate(got, axis=1)

    def in_order(ring, group, y_first):
        x = jnp.stack([ring[d] for d in group]).reshape(-1, NC, NY, NL, SUB, width)
        x = x.transpose((1, 2, 3, 0, 4, 5) if y_first else (1, 3, 2, 0, 4, 5))
        return x.reshape(NC, -1, width)

    pre = lax.all_to_all(pre_act, "col", split_axis=0, concat_axis=0, tiled=True)
    pre = flip_if(roll_to(pre.reshape(NZ, NH, SUB, hid), z), h, 1)

    first = to_relative(out_grad, l, y, c)
    grad = {0: jnp.stack([first, swap_h(first)])}
    for step in (1, 2, 3):
        keep(grad, step, sync(*ring_step(grad, step)))
    x_near, pre, grad[3], grad[-3] = sync(in_order(grad, NEAR, True), pre, grad[3], grad[-3])
    up, down = ring_step(grad, 4)
    away_near = swap_c(bf16(times_trans(x_near[1], w_out)))
    up, down, away_near = sync(up, down, away_near)
    keep(grad, 4, (up, down))
    x_far = in_order(grad, FAR, False)
    away_far = swap_c(bf16(times_trans(x_far[1], w_out)))
    act = to_relative(after(activations, up), l, y, c)
    act_other = swap_h(act)
    part_near = bf16(times_trans(x_near[0], w_out) + f32(away_near)).reshape(NY, NL, -1, hid)
    part_near, away_far, act_other = sync(part_near, away_far, act_other)
    part_far = bf16(times_trans(x_far[0], w_out) + f32(away_far)).reshape(NL, NY, -1, hid)
    act = {0: jnp.stack([act, act_other])}

    got_near = [send_y(part_near[step], step) for step in (2, 1, 3)]
    got_far = swap_l(part_far[1])
    got_act = ring_step(act, 1)
    *got_near, got_far, up, down = sync(*got_near, got_far, *got_act)
    keep(act, 1, (up, down))
    total_near = bf16(f32(part_near[0]) + f32(got_near[0]) + f32(got_near[1]) + f32(got_near[2]))
    total_far = bf16(f32(part_far[0]) + f32(got_far))
    got_far = [send_y(total_far[step], step) for step in (2, 1, 3)]
    got_near = swap_l(total_near[1])
    got_act = ring_step(act, 2)
    *got_far, got_near, up, down = sync(*got_far, got_near, *got_act)
    keep(act, 2, (up, down))

    def hidden_of(group, grad_act):
        slope = gelu_slope(f32(jnp.concatenate([pre[d % NZ] for d in group], axis=0)))
        return bf16(grad_act * slope.reshape(-1, hid))

    hidden_near = hidden_of(NEAR, f32(total_near[0]) + f32(got_near))
    hidden_far = hidden_of(
        FAR, f32(total_far[0]) + f32(got_far[0]) + f32(got_far[1]) + f32(got_far[2])
    )

    got_far = [send_y(hidden_far, step) for step in (3, 2, 1)]
    got_near = swap_l(hidden_near)
    got_act = ring_step(act, 3)
    *got_far, got_near, up, down = sync(*got_far, got_near, *got_act)
    keep(act, 3, (up, down))
    pair_near = jnp.stack([hidden_near, got_near])
    four_far = jnp.stack([hidden_far] + got_far)
    got_near = [send_y(pair_near, step) for step in (3, 2, 1)]
    got_far = swap_l(four_far)
    got_act = ring_step(act, 4)
    *got_near, got_far, up, down = sync(*got_near, got_far, *got_act)
    keep(act, 4, (up, down))
    whole_near = jnp.stack([pair_near] + got_near)
    whole_far = jnp.stack([four_far, got_far])

    def input_shares(group, both, y_first):
        grads = jnp.stack([bf16(times_trans(w, w_in)) for w in both])
        if y_first:
            grads = grads.reshape(NC, NY, NL, -1, SUB, width).transpose(3, 0, 1, 2, 4, 5)
        else:
            grads = grads.reshape(NC, NL, NY, -1, SUB, width).transpose(3, 0, 2, 1, 4, 5)
        grads = grads.reshape(len(group), NH, TOK, width)
        return {d: grads[i] for i, d in enumerate(group)}

    both_far = [w.reshape(-1, hid) for w in (whole_far, swap_c(whole_far))]
    both_near = [w.reshape(-1, hid) for w in (whole_near, swap_c(whole_near))]
    share = {**input_shares(FAR, both_far, False), **input_shares(NEAR, both_near, True)}

    up, down = sync(send_z(share[4][:, :mid], 1), send_z(share[4][:, mid:], -1))
    rest = jnp.zeros_like(up)
    up = jnp.concatenate([up, rest], axis=1)
    down = jnp.concatenate([rest, down], axis=1)
    for d in (3, 2, 1):
        up = bf16(f32(share[d]) + f32(up))
        down = bf16(f32(share[-d]) + f32(down))
        up, down = sync(up, down)
        up, down = sync(send_z(up, 1), send_z(down, -1))
    last = f32(share[0]) + f32(up) + f32(down)
    last = bf16(last[0] + f32(swap_h(bf16(last[1]))))
    grad_input = from_relative(last, l, y, c)

    w_grad = trans_times(
        in_order(act, FAR, False).reshape(-1, width), jnp.concatenate(both_far, axis=0)
    )
    w_grad = w_grad + trans_times(
        in_order(act, NEAR, True).reshape(-1, width), jnp.concatenate(both_near, axis=0)
    )
    return (grad_input, bf16(w_grad))


def solution(mesh):
    in_specs = (P("row", "col"), P("row", "col"), P("col", "row"), P("col", "row"), P("row", "col"))
    out_specs = (P("row", "col"), P("col", "row"))
    return jax.shard_map(local, mesh=mesh, in_specs=in_specs, out_specs=out_specs, check_vma=False)
```

```python
import math

import jax
import jax.numpy as jnp
from jax import lax
from jax.sharding import PartitionSpec as P

NZ, NH, NL, NY, NC = 8, 2, 2, 4, 2
TOK = 128
SUB = 8
NEAR, FAR = (0, 1, -1, 2, -2), (3, -3, 4)


def gelu_slope(hidden):
    coeff = math.sqrt(2.0 / math.pi)
    inner = coeff * (hidden + 0.044715 * hidden * hidden * hidden)
    tanh_val = jnp.tanh(inner)
    return 0.5 * (1.0 + tanh_val) + 0.5 * hidden * (1.0 - tanh_val * tanh_val) * coeff * (
        1.0 + 3.0 * 0.044715 * hidden * hidden
    )


def times_trans(left, right):
    return lax.dot_general(
        left, right, (((left.ndim - 1,), (1,)), ((), ())), preferred_element_type=jnp.float32
    )


def trans_times(left, right):
    return lax.dot_general(
        left, right, (((0,), (0,)), ((), ())), preferred_element_type=jnp.float32
    )


def f32(x):
    return x.astype(jnp.float32)


def bf16(x):
    return x.astype(jnp.bfloat16)


def send_z(x, step):
    pairs = [
        (z * NH + h, (z + step) % NZ * NH + h) for z in range(NZ) for h in range(NH)
    ]
    return lax.ppermute(x, "row", pairs)


def swap_h(x):
    return lax.ppermute(x, "row", [(r, r ^ 1) for r in range(NZ * NH)])


def send_diagonal(x, step):
    pairs = [
        (z * NH + h, (z + step) % NZ * NH + 1 - h) for z in range(NZ) for h in range(NH)
    ]
    return lax.ppermute(x, "row", pairs)


def send_y(x, step):
    pairs = [
        ((l * NY + y) * NC + c, (l * NY + (y + step) % NY) * NC + c)
        for l in range(NL)
        for y in range(NY)
        for c in range(NC)
    ]
    return lax.ppermute(x, "col", pairs)


def swap_l(x):
    return lax.ppermute(x, "col", [(j, j ^ (NY * NC)) for j in range(NL * NY * NC)])


def swap_c(x):
    return lax.ppermute(x, "col", [(j, j ^ 1) for j in range(NL * NY * NC)])


def after(x, *deps):
    return lax.optimization_barrier((x,) + deps)[0]


def roll_to(x, start):
    twice = jnp.concatenate([x, x], axis=0)
    return lax.dynamic_slice_in_dim(twice, start, x.shape[0], axis=0)


def flip_if(x, flag, axis):
    return jnp.where(flag == 1, jnp.flip(x, axis), x)


def to_relative(x, l, y, c):
    x = x.reshape(NL, NY, NC, SUB, -1)
    x = flip_if(flip_if(x, l, 0), c, 2)
    x = roll_to(x.transpose(1, 0, 2, 3, 4), y)
    return x.transpose(2, 0, 1, 3, 4).reshape(TOK, -1)


def from_relative(x, l, y, c):
    x = x.reshape(NC, NY, NL, SUB, -1).transpose(1, 2, 0, 3, 4)
    x = roll_to(x, (NY - y) % NY).transpose(1, 0, 2, 3, 4)
    return flip_if(flip_if(x, l, 0), c, 2).reshape(TOK, -1)


def sync(*xs):
    return lax.optimization_barrier(xs)


def local(activations, out_grad, pre_act, w_in, w_out):
    row, col = lax.axis_index("row"), lax.axis_index("col")
    z, h = row // NH, row % NH
    l, y, c = col // (NY * NC), col // NC % NY, col % NC
    width, hid = activations.shape[1], w_in.shape[1]
    mid = TOK // 2

    def ring_step(ring, step):
        if step < 4:
            return send_z(ring[1 - step], 1), send_z(ring[step - 1], -1)
        return send_z(ring[-3][:, :mid], 1), send_z(ring[3][:, mid:], -1)

    def keep(ring, step, got):
        if step < 4:
            ring[-step], ring[step] = got
        else:
            ring[4] = jnp.concatenate(got, axis=1)

    def in_order(ring, group, y_first):
        x = jnp.stack([ring[d] for d in group]).reshape(-1, NC, NY, NL, SUB, width)
        x = x.transpose((1, 2, 3, 0, 4, 5) if y_first else (1, 3, 2, 0, 4, 5))
        return x.reshape(NC, -1, width)

    pre = lax.all_to_all(pre_act, "col", split_axis=0, concat_axis=0, tiled=True)
    pre = flip_if(roll_to(pre.reshape(NZ, NH, SUB, hid), z), h, 1)

    first = to_relative(out_grad, l, y, c)
    grad = {0: jnp.stack([first, swap_h(first)])}
    up, down = ring_step(grad, 1)
    act = to_relative(activations, l, y, c)
    up, down, act = sync(up, down, act)
    keep(grad, 1, (up, down))
    act_other = swap_h(act)
    keep(grad, 2, sync(*ring_step(grad, 2)))
    up, down = ring_step(grad, 3)
    x_near, pre, up, down, act_other = sync(in_order(grad, NEAR, True), pre, up, down, act_other)
    keep(grad, 3, (up, down))
    up, down = ring_step(grad, 4)
    away_near = swap_c(bf16(times_trans(x_near[1], w_out)))
    part_near = bf16(times_trans(x_near[0], w_out) + f32(away_near))
    up, down, part_near, act = sync(up, down, part_near, jnp.stack([act, act_other]))
    keep(grad, 4, (up, down))
    x_far = in_order(grad, FAR, False)
    away_far = swap_c(bf16(times_trans(x_far[1], w_out)))
    part_near = part_near.reshape(NY, NL, -1, hid)
    part_far = bf16(times_trans(x_far[0], w_out) + f32(away_far)).reshape(NL, NY, -1, hid)
    act = {0: act}

    got_near = [send_y(part_near[step], step) for step in (2, 1, 3)]
    got_far = swap_l(part_far[1])
    keep(act, 1, sync(*ring_step(act, 1)))
    got_act = ring_step(act, 2)
    *got_near, got_far, up, down = sync(*got_near, got_far, *got_act)
    keep(act, 2, (up, down))
    total_near = bf16(f32(part_near[0]) + f32(got_near[0]) + f32(got_near[1]) + f32(got_near[2]))
    total_far = bf16(f32(part_far[0]) + f32(got_far))
    got_far = [send_y(total_far[step], step) for step in (2, 1, 3)]
    got_near = swap_l(total_near[1])
    *got_far, got_near = sync(*got_far, got_near)

    def hidden_of(group, grad_act):
        slope = gelu_slope(f32(jnp.concatenate([pre[d % NZ] for d in group], axis=0)))
        return bf16(grad_act * slope.reshape(-1, hid))

    hidden_near = hidden_of(NEAR, f32(total_near[0]) + f32(got_near))
    hidden_far = hidden_of(
        FAR, f32(total_far[0]) + f32(got_far[0]) + f32(got_far[1]) + f32(got_far[2])
    )

    got_far = [send_y(hidden_far, step) for step in (3, 2, 1)]
    got_near = swap_l(hidden_near)
    *got_far, got_near = sync(*got_far, got_near)
    pair_near = jnp.stack([hidden_near, got_near])
    four_far = jnp.stack([hidden_far] + got_far)
    got_near = [send_y(pair_near, step) for step in (3, 2, 1)]
    got_far = swap_l(four_far)
    keep(act, 3, sync(*ring_step(act, 3)))
    got_act = ring_step(act, 4)
    *got_near, got_far, up, down = sync(*got_near, got_far, *got_act)
    keep(act, 4, (up, down))
    whole_near = jnp.stack([pair_near] + got_near)
    whole_far = jnp.stack([four_far, got_far])

    def input_shares(group, both, y_first):
        grads = jnp.stack([bf16(times_trans(w, w_in)) for w in both])
        if y_first:
            grads = grads.reshape(NC, NY, NL, -1, SUB, width).transpose(3, 0, 1, 2, 4, 5)
        else:
            grads = grads.reshape(NC, NL, NY, -1, SUB, width).transpose(3, 0, 2, 1, 4, 5)
        grads = grads.reshape(len(group), NH, TOK, width)
        return {d: grads[i] for i, d in enumerate(group)}

    both_far = [w.reshape(-1, hid) for w in (whole_far, swap_c(whole_far))]
    share = input_shares(FAR, both_far, False)
    both_near = [w.reshape(-1, hid) for w in (after(whole_near, share[4]), swap_c(whole_near))]
    share = {**share, **input_shares(NEAR, both_near, True)}

    up, down = sync(send_z(share[4][:, :mid], 1), send_z(share[4][:, mid:], -1))
    rest = jnp.zeros_like(up)
    up = jnp.concatenate([up, rest], axis=1)
    down = jnp.concatenate([rest, down], axis=1)
    crossed = swap_h(share[0][1])
    for d in (3, 2):
        up = bf16(f32(share[d]) + f32(up))
        down = bf16(f32(share[-d]) + f32(down))
        up, down = sync(up, down)
        up, down, crossed = sync(send_z(up, 1), send_z(down, -1), crossed)
    up = bf16(f32(share[1]) + f32(up))
    down = bf16(f32(share[-1]) + f32(down))
    up, down = sync(up, down)
    last = f32(share[0][0]) + f32(crossed)
    got = sync(
        send_z(up[0], 1), send_diagonal(up[1], 1), send_z(down[0], -1), send_diagonal(down[1], -1)
    )
    for term in got:
        last = last + f32(term)
    grad_input = from_relative(bf16(last), l, y, c)

    w_grad = trans_times(
        in_order(act, FAR, False).reshape(-1, width), jnp.concatenate(both_far, axis=0)
    )
    w_grad = w_grad + trans_times(
        in_order(act, NEAR, True).reshape(-1, width), jnp.concatenate(both_near, axis=0)
    )
    return (grad_input, bf16(w_grad))


def solution(mesh):
    in_specs = (P("row", "col"), P("row", "col"), P("col", "row"), P("col", "row"), P("row", "col"))
    out_specs = (P("row", "col"), P("col", "row"))
    return jax.shard_map(local, mesh=mesh, in_specs=in_specs, out_specs=out_specs, check_vma=False)
```

```python
import math

import jax
import jax.numpy as jnp
from jax import lax
from jax.sharding import PartitionSpec as P

NZ, NH, NL, NY, NC = 8, 2, 2, 4, 2
TOK = 128
SUB = 8
NEAR, FAR = (0, 1, -1, 2, -2), (3, -3, 4)


def gelu_slope(hidden):
    coeff = math.sqrt(2.0 / math.pi)
    inner = coeff * (hidden + 0.044715 * hidden * hidden * hidden)
    tanh_val = jnp.tanh(inner)
    return 0.5 * (1.0 + tanh_val) + 0.5 * hidden * (1.0 - tanh_val * tanh_val) * coeff * (
        1.0 + 3.0 * 0.044715 * hidden * hidden
    )


def times_trans(left, right):
    return lax.dot_general(
        left, right, (((left.ndim - 1,), (1,)), ((), ())), preferred_element_type=jnp.float32
    )


def trans_times(left, right):
    return lax.dot_general(
        left, right, (((0,), (0,)), ((), ())), preferred_element_type=jnp.float32
    )


def f32(x):
    return x.astype(jnp.float32)


def bf16(x):
    return x.astype(jnp.bfloat16)


def send_z(x, step):
    pairs = [
        (z * NH + h, (z + step) % NZ * NH + h) for z in range(NZ) for h in range(NH)
    ]
    return lax.ppermute(x, "row", pairs)


def swap_h(x):
    return lax.ppermute(x, "row", [(r, r ^ 1) for r in range(NZ * NH)])


def send_diagonal(x, step):
    pairs = [
        (z * NH + h, (z + step) % NZ * NH + 1 - h) for z in range(NZ) for h in range(NH)
    ]
    return lax.ppermute(x, "row", pairs)


def send_y(x, step):
    pairs = [
        ((l * NY + y) * NC + c, (l * NY + (y + step) % NY) * NC + c)
        for l in range(NL)
        for y in range(NY)
        for c in range(NC)
    ]
    return lax.ppermute(x, "col", pairs)


def swap_l(x):
    return lax.ppermute(x, "col", [(j, j ^ (NY * NC)) for j in range(NL * NY * NC)])


def swap_c(x):
    return lax.ppermute(x, "col", [(j, j ^ 1) for j in range(NL * NY * NC)])


def after(x, *deps):
    return lax.optimization_barrier((x,) + deps)[0]


def roll_to(x, start):
    twice = jnp.concatenate([x, x], axis=0)
    return lax.dynamic_slice_in_dim(twice, start, x.shape[0], axis=0)


def flip_if(x, flag, axis):
    return jnp.where(flag == 1, jnp.flip(x, axis), x)


def to_relative(x, l, y, c):
    x = x.reshape(NL, NY, NC, SUB, -1)
    x = flip_if(flip_if(x, l, 0), c, 2)
    x = roll_to(x.transpose(1, 0, 2, 3, 4), y)
    return x.transpose(2, 0, 1, 3, 4).reshape(TOK, -1)


def from_relative(x, l, y, c):
    x = x.reshape(NC, NY, NL, SUB, -1).transpose(1, 2, 0, 3, 4)
    x = roll_to(x, (NY - y) % NY).transpose(1, 0, 2, 3, 4)
    return flip_if(flip_if(x, l, 0), c, 2).reshape(TOK, -1)


def sync(*xs):
    return lax.optimization_barrier(xs)


def local(activations, out_grad, pre_act, w_in, w_out):
    row, col = lax.axis_index("row"), lax.axis_index("col")
    z, h = row // NH, row % NH
    l, y, c = col // (NY * NC), col // NC % NY, col % NC
    width, hid = activations.shape[1], w_in.shape[1]
    mid = TOK // 2

    def ring_step(ring, step):
        if step < 4:
            return send_z(ring[1 - step], 1), send_z(ring[step - 1], -1)
        return send_z(ring[-3][:, :mid], 1), send_z(ring[3][:, mid:], -1)

    def keep(ring, step, got):
        if step < 4:
            ring[-step], ring[step] = got
        else:
            ring[4] = jnp.concatenate(got, axis=1)

    def in_order(ring, group, y_first):
        x = jnp.stack([ring[d] for d in group]).reshape(-1, NC, NY, NL, SUB, width)
        x = x.transpose((1, 2, 3, 0, 4, 5) if y_first else (1, 3, 2, 0, 4, 5))
        return x.reshape(NC, -1, width)

    pre = lax.all_to_all(pre_act, "col", split_axis=0, concat_axis=0, tiled=True)
    pre = flip_if(roll_to(pre.reshape(NZ, NH, SUB, hid), z), h, 1)

    first = to_relative(out_grad, l, y, c)
    grad = {0: jnp.stack([first, swap_h(first)])}
    keep(grad, 1, sync(*ring_step(grad, 1)))
    act = to_relative(after(activations, grad[1]), l, y, c)
    act_other = swap_h(act)
    keep(grad, 2, sync(*ring_step(grad, 2)))
    up, down = ring_step(grad, 3)
    x_near, pre, up, down, act_other = sync(in_order(grad, NEAR, True), pre, up, down, act_other)
    keep(grad, 3, (up, down))
    up, down = ring_step(grad, 4)
    away_near = swap_c(bf16(times_trans(x_near[1], w_out)))
    part_near = bf16(times_trans(x_near[0], w_out) + f32(away_near))
    up, down, part_near, act = sync(up, down, part_near, jnp.stack([act, act_other]))
    keep(grad, 4, (up, down))
    x_far = in_order(grad, FAR, False)
    away_far = swap_c(bf16(times_trans(x_far[1], w_out)))
    part_near = part_near.reshape(NY, NL, -1, hid)
    part_far = bf16(times_trans(x_far[0], w_out) + f32(away_far)).reshape(NL, NY, -1, hid)
    act = {0: act}

    got_near = [send_y(part_near[step], step) for step in (2, 1, 3)]
    got_far = swap_l(part_far[1])
    keep(act, 1, sync(*ring_step(act, 1)))
    got_act = ring_step(act, 2)
    *got_near, got_far, up, down = sync(*got_near, got_far, *got_act)
    keep(act, 2, (up, down))
    total_near = bf16(f32(part_near[0]) + f32(got_near[0]) + f32(got_near[1]) + f32(got_near[2]))
    total_far = bf16(f32(part_far[0]) + f32(got_far))
    got_far = [send_y(total_far[step], step) for step in (2, 1, 3)]
    got_near = swap_l(total_near[1])
    *got_far, got_near = sync(*got_far, got_near)

    def hidden_of(group, grad_act):
        slope = gelu_slope(f32(jnp.concatenate([pre[d % NZ] for d in group], axis=0)))
        return bf16(grad_act * slope.reshape(-1, hid))

    hidden_near = hidden_of(NEAR, f32(total_near[0]) + f32(got_near))
    hidden_far = hidden_of(
        FAR, f32(total_far[0]) + f32(got_far[0]) + f32(got_far[1]) + f32(got_far[2])
    )

    got_far = [send_y(hidden_far, step) for step in (3, 2, 1)]
    got_near = swap_l(hidden_near)
    *got_far, got_near = sync(*got_far, got_near)
    pair_near = jnp.stack([hidden_near, got_near])
    four_far = jnp.stack([hidden_far] + got_far)
    got_near = [send_y(pair_near, step) for step in (3, 2, 1)]
    got_far = swap_l(four_far)
    keep(act, 3, sync(*ring_step(act, 3)))
    got_act = ring_step(act, 4)
    *got_near, got_far, up, down = sync(*got_near, got_far, *got_act)
    keep(act, 4, (up, down))
    whole_near = jnp.stack([pair_near] + got_near)
    whole_far = jnp.stack([four_far, got_far])

    def input_shares(group, both, y_first):
        grads = jnp.stack([bf16(times_trans(w, w_in)) for w in both])
        if y_first:
            grads = grads.reshape(NC, NY, NL, -1, SUB, width).transpose(3, 0, 1, 2, 4, 5)
        else:
            grads = grads.reshape(NC, NL, NY, -1, SUB, width).transpose(3, 0, 2, 1, 4, 5)
        grads = grads.reshape(len(group), NH, TOK, width)
        return {d: grads[i] for i, d in enumerate(group)}

    both_far = [w.reshape(-1, hid) for w in (whole_far, swap_c(whole_far))]
    share = input_shares(FAR, both_far, False)
    both_near = [w.reshape(-1, hid) for w in (after(whole_near, share[4]), swap_c(whole_near))]
    share = {**share, **input_shares(NEAR, both_near, True)}

    up, down = sync(send_z(share[4][:, :mid], 1), send_z(share[4][:, mid:], -1))
    rest = jnp.zeros_like(up)
    up = jnp.concatenate([up, rest], axis=1)
    down = jnp.concatenate([rest, down], axis=1)
    crossed = swap_h(share[0][1])
    for d in (3, 2):
        up = bf16(f32(share[d]) + f32(up))
        down = bf16(f32(share[-d]) + f32(down))
        up, down = sync(up, down)
        up, down, crossed = sync(send_z(up, 1), send_z(down, -1), crossed)
    up = bf16(f32(share[1]) + f32(up))
    down = bf16(f32(share[-1]) + f32(down))
    up, down = sync(up, down)
    last = f32(share[0][0]) + f32(crossed)
    got = sync(
        send_z(up[0], 1), send_diagonal(up[1], 1), send_z(down[0], -1), send_diagonal(down[1], -1)
    )
    for term in got:
        last = last + f32(term)
    grad_input = from_relative(bf16(last), l, y, c)

    w_grad = trans_times(
        in_order(act, FAR, False).reshape(-1, width), jnp.concatenate(both_far, axis=0)
    )
    w_grad = w_grad + trans_times(
        in_order(act, NEAR, True).reshape(-1, width), jnp.concatenate(both_near, axis=0)
    )
    return (grad_input, bf16(w_grad))


def solution(mesh):
    in_specs = (P("row", "col"), P("row", "col"), P("col", "row"), P("col", "row"), P("row", "col"))
    out_specs = (P("row", "col"), P("col", "row"))
    return jax.shard_map(local, mesh=mesh, in_specs=in_specs, out_specs=out_specs, check_vma=False)
```

```python
import math

import jax
import jax.numpy as jnp
from jax import lax
from jax.sharding import PartitionSpec as P

NZ, NH, NL, NY, NC = 8, 2, 2, 4, 2
TOK = 128
SUB = 8
NEAR, FAR = (0, 1, -1, 2, -2), (3, -3, 4)


def gelu_slope(hidden):
    coeff = math.sqrt(2.0 / math.pi)
    inner = coeff * (hidden + 0.044715 * hidden * hidden * hidden)
    tanh_val = jnp.tanh(inner)
    return 0.5 * (1.0 + tanh_val) + 0.5 * hidden * (1.0 - tanh_val * tanh_val) * coeff * (
        1.0 + 3.0 * 0.044715 * hidden * hidden
    )


def times_trans(left, right):
    return lax.dot_general(
        left, right, (((left.ndim - 1,), (1,)), ((), ())), preferred_element_type=jnp.float32
    )


def trans_times(left, right):
    return lax.dot_general(
        left, right, (((0,), (0,)), ((), ())), preferred_element_type=jnp.float32
    )


def f32(x):
    return x.astype(jnp.float32)


def bf16(x):
    return x.astype(jnp.bfloat16)


def send_z(x, step):
    pairs = [
        (z * NH + h, (z + step) % NZ * NH + h) for z in range(NZ) for h in range(NH)
    ]
    return lax.ppermute(x, "row", pairs)


def swap_h(x):
    return lax.ppermute(x, "row", [(r, r ^ 1) for r in range(NZ * NH)])


def send_diagonal(x, step):
    pairs = [
        (z * NH + h, (z + step) % NZ * NH + 1 - h) for z in range(NZ) for h in range(NH)
    ]
    return lax.ppermute(x, "row", pairs)


def send_y(x, step):
    pairs = [
        ((l * NY + y) * NC + c, (l * NY + (y + step) % NY) * NC + c)
        for l in range(NL)
        for y in range(NY)
        for c in range(NC)
    ]
    return lax.ppermute(x, "col", pairs)


def swap_l(x):
    return lax.ppermute(x, "col", [(j, j ^ (NY * NC)) for j in range(NL * NY * NC)])


def swap_c(x):
    return lax.ppermute(x, "col", [(j, j ^ 1) for j in range(NL * NY * NC)])


def after(x, *deps):
    return lax.optimization_barrier((x,) + deps)[0]


def roll_to(x, start):
    twice = jnp.concatenate([x, x], axis=0)
    return lax.dynamic_slice_in_dim(twice, start, x.shape[0], axis=0)


def flip_if(x, flag, axis):
    return jnp.where(flag == 1, jnp.flip(x, axis), x)


def to_relative(x, l, y, c):
    x = x.reshape(NL, NY, NC, SUB, -1)
    x = flip_if(flip_if(x, l, 0), c, 2)
    x = roll_to(x.transpose(1, 0, 2, 3, 4), y)
    return x.transpose(2, 0, 1, 3, 4).reshape(TOK, -1)


def from_relative(x, l, y, c):
    x = x.reshape(NC, NY, NL, SUB, -1).transpose(1, 2, 0, 3, 4)
    x = roll_to(x, (NY - y) % NY).transpose(1, 0, 2, 3, 4)
    return flip_if(flip_if(x, l, 0), c, 2).reshape(TOK, -1)


def sync(*xs):
    return lax.optimization_barrier(xs)


def local(activations, out_grad, pre_act, w_in, w_out):
    row, col = lax.axis_index("row"), lax.axis_index("col")
    z, h = row // NH, row % NH
    l, y, c = col // (NY * NC), col // NC % NY, col % NC
    width, hid = activations.shape[1], w_in.shape[1]
    mid = TOK // 2

    def ring_step(ring, step):
        if step < 4:
            return send_z(ring[1 - step], 1), send_z(ring[step - 1], -1)
        return send_z(ring[-3][:, :mid], 1), send_z(ring[3][:, mid:], -1)

    def keep(ring, step, got):
        if step < 4:
            ring[-step], ring[step] = got
        else:
            ring[4] = jnp.concatenate(got, axis=1)

    def in_order(ring, group, y_first):
        x = jnp.stack([ring[d] for d in group]).reshape(-1, NC, NY, NL, SUB, width)
        x = x.transpose((1, 2, 3, 0, 4, 5) if y_first else (1, 3, 2, 0, 4, 5))
        return x.reshape(NC, -1, width)

    pre = lax.all_to_all(pre_act, "col", split_axis=0, concat_axis=0, tiled=True)
    pre = flip_if(roll_to(pre.reshape(NZ, NH, SUB, hid), z), h, 1)

    first = to_relative(out_grad, l, y, c)
    grad = {0: jnp.stack([first, swap_h(first)])}
    keep(grad, 1, sync(*ring_step(grad, 1)))
    act = to_relative(after(activations, grad[1]), l, y, c)
    act_other = swap_h(act)
    keep(grad, 2, sync(*ring_step(grad, 2)))
    up, down = ring_step(grad, 3)
    x_near, pre, up, down, act_other = sync(in_order(grad, NEAR, True), pre, up, down, act_other)
    keep(grad, 3, (up, down))
    up, down = ring_step(grad, 4)
    away_near = swap_c(bf16(times_trans(x_near[1], w_out)))
    part_near = bf16(times_trans(x_near[0], w_out) + f32(away_near))
    up, down, part_near, act = sync(up, down, part_near, jnp.stack([act, act_other]))
    keep(grad, 4, (up, down))
    x_far = in_order(grad, FAR, False)
    away_far = swap_c(bf16(times_trans(x_far[1], w_out)))
    part_near = part_near.reshape(NY, NL, -1, hid)
    part_far = bf16(times_trans(x_far[0], w_out) + f32(away_far)).reshape(NL, NY, -1, hid)
    act = {0: act}

    got_near = [send_y(part_near[step], step) for step in (2, 1, 3)]
    got_far = swap_l(part_far[1])
    keep(act, 1, sync(*ring_step(act, 1)))
    got_act = ring_step(act, 2)
    *got_near, got_far, up, down = sync(*got_near, got_far, *got_act)
    keep(act, 2, (up, down))
    total_near = bf16(f32(part_near[0]) + f32(got_near[0]) + f32(got_near[1]) + f32(got_near[2]))
    total_far = bf16(f32(part_far[0]) + f32(got_far))
    got_far = [send_y(total_far[step], step) for step in (2, 1, 3)]
    got_near = swap_l(total_near[1])
    *got_far, got_near = sync(*got_far, got_near)

    def hidden_of(group, grad_act):
        slope = gelu_slope(f32(jnp.concatenate([pre[d % NZ] for d in group], axis=0)))
        return bf16(grad_act * slope.reshape(-1, hid))

    hidden_near = hidden_of(NEAR, f32(total_near[0]) + f32(got_near))
    hidden_far = hidden_of(
        FAR, f32(total_far[0]) + f32(got_far[0]) + f32(got_far[1]) + f32(got_far[2])
    )

    got_far = [send_y(hidden_far, step) for step in (3, 2, 1)]
    got_near = swap_l(hidden_near)
    *got_far, got_near = sync(*got_far, got_near)
    pair_near = jnp.stack([hidden_near, got_near])
    four_far = jnp.stack([hidden_far] + got_far)
    got_near = [send_y(pair_near, step) for step in (3, 2, 1)]
    got_far = swap_l(four_far)
    keep(act, 3, sync(*ring_step(act, 3)))
    got_act = ring_step(act, 4)
    *got_near, got_far, up, down = sync(*got_near, got_far, *got_act)
    keep(act, 4, (up, down))
    whole_near = jnp.stack([pair_near] + got_near)
    whole_far = jnp.stack([four_far, got_far])

    def input_shares(group, both, y_first):
        grads = jnp.stack([bf16(times_trans(w, w_in)) for w in both])
        if y_first:
            grads = grads.reshape(NC, NY, NL, -1, SUB, width).transpose(3, 0, 1, 2, 4, 5)
        else:
            grads = grads.reshape(NC, NL, NY, -1, SUB, width).transpose(3, 0, 2, 1, 4, 5)
        grads = grads.reshape(len(group), NH, TOK, width)
        return {d: grads[i] for i, d in enumerate(group)}

    both_far = [w.reshape(-1, hid) for w in (whole_far, swap_c(whole_far))]
    share = input_shares(FAR, both_far, False)
    both_near = [w.reshape(-1, hid) for w in (after(whole_near, share[4]), swap_c(whole_near))]
    share = {**share, **input_shares(NEAR, both_near, True)}

    up, down = sync(send_z(share[4][:, :mid], 1), send_z(share[4][:, mid:], -1))
    rest = jnp.zeros_like(up)
    up = jnp.concatenate([up, rest], axis=1)
    down = jnp.concatenate([rest, down], axis=1)
    crossed = swap_h(share[0][1])
    for d in (3, 2):
        up = bf16(f32(share[d]) + f32(up))
        down = bf16(f32(share[-d]) + f32(down))
        up, down = sync(up, down)
        up, down = sync(send_z(up, 1), send_z(down, -1))
    up = bf16(f32(share[1]) + f32(up))
    down = bf16(f32(share[-1]) + f32(down))
    up, down, crossed = sync(up, down, crossed)
    last = f32(share[0][0]) + f32(crossed)
    got = sync(
        send_z(up[0], 1), send_diagonal(up[1], 1), send_z(down[0], -1), send_diagonal(down[1], -1)
    )
    for term in got:
        last = last + f32(term)
    grad_input = from_relative(bf16(last), l, y, c)

    w_grad = trans_times(
        in_order(act, FAR, False).reshape(-1, width), jnp.concatenate(both_far, axis=0)
    )
    w_grad = w_grad + trans_times(
        in_order(act, NEAR, True).reshape(-1, width), jnp.concatenate(both_near, axis=0)
    )
    return (grad_input, bf16(w_grad))


def solution(mesh):
    in_specs = (P("row", "col"), P("row", "col"), P("col", "row"), P("col", "row"), P("row", "col"))
    out_specs = (P("row", "col"), P("col", "row"))
    return jax.shard_map(local, mesh=mesh, in_specs=in_specs, out_specs=out_specs, check_vma=False)
```
